32 devices in a mesh: req: 16 (over z, y, core), tp: 2 (over x).
Axes of the slice: x: 2, y: 2, z: 4, core: 2. Of those that a mesh axis runs over, the one named last changes fastest.
Arguments:
- tokens: bfloat16 [16, 512, 2048], P('req', 'tp'), may hold values from -6 to 6
- w_q: bfloat16 [2048, 1024], P(None, 'tp')
- w_k: bfloat16 [2048, 1024], P(None, 'tp')
- w_v: bfloat16 [2048, 1024], P(None, 'tp'), may hold values from -0.125 to 0.125
- w_o: bfloat16 [1024, 2048], P('tp'), may hold values from -0.1875 to 0.1875
- q_gain: float32 [1024], P('tp'), may hold values from 0.1 to 1.9
- k_gain: float32 [1024], P('tp'), may hold values from 0.1 to 1.9
- out_gain: float32 [2048], replicated, may hold values from 0.1 to 1.9
- cache_lens: int32 [16], P('req'), may hold values from 512 to 4096, as said below
- group_ids: int32 [16], replicated, may hold values from 0 to 7
- prefix_cache: bfloat16 [8, 256, 2048], P(None, 'req', 'tp'), may hold values from -6 to 6
- cache_rows: bfloat16 [16, 4096, 2048], P('req', None, 'tp'), may hold values from -105 to 105
Outputs:
- hidden: bfloat16 [16, 512, 2048], P('req', 'tp')
- appended: bfloat16 [16, 512, 2048], P('req', None, 'tp')
The draws below stay inside these ranges and needn't reach their ends.
Inputs may be any that keep to these rules, and one draw needn't show every extreme that they name: `cache_lens`: every draw holds a request with exactly 4096 cached positions.
All inputs are finite; a program needn't handle non-finite values.
Results may differ from the reference program's by a relative error of at most 0.013.
Values may be sent and summed in bfloat16 or wider, within the bound.
A program may use at most 64 MiB of HBM per device.

```python
import jax
import jax.numpy as jnp
from jax import lax

D = 2048
HEADS = 8
HD = 128
GROUPS = 8
NEW = 512
CMAX = 4096
PREFIX = 256
REQS = 16
N_TP = 2


def head_ramp():
    return jnp.repeat(0.6 * jnp.power(3.0, jnp.arange(HEADS, dtype=jnp.float32) / (HEADS - 1)), HD)


def ramped_weight(key):
    base = jax.random.normal(key, (D, HEADS * HD), jnp.float32)
    return (base * D ** (-0.5) * head_ramp()[None, :]).astype(jnp.bfloat16)


def draw_w_q(key, part):
    return ramped_weight(jax.random.fold_in(key, 11))


def draw_w_k(key, part):
    return ramped_weight(jax.random.fold_in(key, 12))


def draw_cache_lens(key, part):
    lens = jax.random.randint(jax.random.fold_in(key, 21), (REQS,), CMAX // 8, CMAX + 1)
    spot = jax.random.randint(jax.random.fold_in(key, 22), (), 0, REQS)
    return lens.at[spot].set(CMAX).astype(jnp.int32)


def draw_cache_rows(key, part):
    full_shape = (REQS, CMAX, HEADS, 2, HD)
    subkey = jax.random.fold_in(key, 31)
    base = jnp.clip(jax.random.normal(subkey, full_shape, jnp.float32), -6.0, 6.0)
    return base.reshape(REQS, CMAX, HEADS * 2 * HD).astype(jnp.bfloat16)


def touch_ends(array, own_key, least, top_value):
    place = [jax.random.randint(jax.random.fold_in(own_key, axis), (), 0, length) for axis, length in enumerate(array.shape)]
    main_axis = array.shape.index(max(array.shape))
    beside = place[:main_axis] + [(place[main_axis] + 1) % array.shape[main_axis]] + place[main_axis + 1:]
    return array.at[tuple(place)].set(least).at[tuple(beside)].set(top_value)


def level_of(key, extent, pieces, low, top_value):
    def one(position, shards_of):
        steps = jax.random.uniform(jax.random.fold_in(jax.random.fold_in(key, 6), position), (shards_of,), jnp.float32, low / len(pieces), top_value / len(pieces))
        return jnp.repeat(jnp.exp(steps), extent[position] // shards_of).reshape((-1,) + (1,) * (len(extent) - position - 1))

    factor_of = one(*pieces[0])
    for cut in pieces[1:]:
        factor_of = factor_of * one(*cut)
    return factor_of


def gaussian(stream_key, extent, width, most, cuts=(), kind=jnp.bfloat16):
    array = width * jax.random.normal(stream_key, extent, jnp.float32)
    if cuts:
        array = array * level_of(stream_key, extent, cuts, -0.22, 0.18)
    return jnp.clip(array, -most, most).astype(kind)


def setup_inputs(seed: int = 0) -> dict:
    keys = jax.random.split(jax.random.key(seed), 13)
    tokens = gaussian(keys[0], (REQS, NEW, D), 1.0, 6.0, ((0, 16), (1, 2)))
    w_q = draw_w_q(jax.random.fold_in(keys[12], 71), 0)
    w_k = draw_w_k(jax.random.fold_in(keys[12], 71), 0)
    w_v = gaussian(keys[3], (D, HEADS * HD), D ** -0.5, 0.125, ((1, 2),))
    w_o = gaussian(keys[4], (HEADS * HD, D), (HEADS * HD) ** -0.5, 0.1875, ((0, 2),))
    q_gain = jnp.clip(1.0 + 0.18 * jax.random.normal(keys[5], (HEADS * HD,), jnp.float32), 0.1, 1.9)
    k_gain = jnp.clip(1.0 + 0.18 * jax.random.normal(keys[6], (HEADS * HD,), jnp.float32), 0.1, 1.9)
    out_gain = jnp.clip(1.0 + 0.18 * jax.random.normal(keys[7], (D,), jnp.float32), 0.1, 1.9)
    cache_lens = draw_cache_lens(jax.random.fold_in(keys[12], 71), 0)
    group_ids = touch_ends(jax.random.randint(keys[9], (REQS,), 0, GROUPS), jax.random.fold_in(keys[9], 1), 0, GROUPS - 1).astype(jnp.int32)
    prefix_cache = gaussian(keys[10], (GROUPS, PREFIX, HEADS * 2 * HD), 1.0, 6.0, ((1, 16), (2, 2)))
    cache_rows = draw_cache_rows(jax.random.fold_in(keys[12], 71), 0)
    return dict(tokens=tokens, w_q=w_q, w_k=w_k, w_v=w_v, w_o=w_o, q_gain=q_gain, k_gain=k_gain, out_gain=out_gain, cache_lens=cache_lens, group_ids=group_ids, prefix_cache=prefix_cache, cache_rows=cache_rows)


def rotate(values_in, positions):
    half_dim = values_in.shape[-1] // 2
    exponent = jnp.arange(half_dim, dtype=jnp.float32) * (-2.0 / values_in.shape[-1])
    inverse = jnp.power(jnp.float32(500000.0), exponent)
    angles = positions[:, None] * inverse[None, :]
    cosine = jnp.cos(angles)[:, None, :]
    sine_part = jnp.sin(angles)[:, None, :]
    first_half = values_in[..., :half_dim]
    second_half = values_in[..., half_dim:]
    return jnp.concatenate([first_half * cosine - second_half * sine_part, second_half * cosine + first_half * sine_part], -1)

def rms_scale(values_in, gain_vector):
    mean_sq = lax.optimization_barrier(jnp.mean(values_in * values_in, axis=-1, keepdims=True))
    return values_in * lax.rsqrt(mean_sq + 1e-06) * gain_vector

def reference(tokens, w_q, w_k, w_v, w_o, q_gain, k_gain, out_gain, cache_lens, group_ids, prefix_cache, cache_rows):
    score_scale = HD ** (-0.5)
    group_cols = HEADS // N_TP * HD

    def one_request(inputs):
        rows_in, length, group_id, cached = inputs
        queries = rms_scale(jnp.dot(rows_in, w_q, preferred_element_type=jnp.float32), q_gain)
        keys_new = rms_scale(jnp.dot(rows_in, w_k, preferred_element_type=jnp.float32), k_gain)
        values_new = jnp.dot(rows_in, w_v, preferred_element_type=jnp.float32)
        positions = (PREFIX + length + jnp.arange(NEW, dtype=jnp.int32)).astype(jnp.float32)
        q_rot = rotate(queries.reshape(NEW, HEADS, HD), positions).astype(jnp.bfloat16)
        k_rot = rotate(keys_new.reshape(NEW, HEADS, HD), positions).astype(jnp.bfloat16)
        v_new = values_new.reshape(NEW, HEADS, HD).astype(jnp.bfloat16)
        appended = jnp.stack([k_rot, v_new], axis=2).reshape(NEW, HEADS * 2 * HD)
        shared = lax.dynamic_index_in_dim(prefix_cache, group_id, 0, keepdims=False).reshape(PREFIX, HEADS, 2, HD)
        private = cached.reshape(CMAX, HEADS, 2, HD)
        keys_all = jnp.concatenate([shared[:, :, 0], private[:, :, 0], k_rot], 0)
        values_all = jnp.concatenate([shared[:, :, 1], private[:, :, 1], v_new], 0)
        query_pos = jnp.arange(NEW, dtype=jnp.int32)[:, None]
        cache_pos = jnp.arange(CMAX, dtype=jnp.int32)[None, :]
        visible = jnp.concatenate([jnp.ones((NEW, PREFIX), dtype=bool), jnp.broadcast_to(cache_pos < length, (NEW, CMAX)), jnp.arange(NEW, dtype=jnp.int32)[None, :] <= query_pos], 1)
        scores = jnp.einsum('qhd,khd->hqk', q_rot.astype(jnp.float32), keys_all.astype(jnp.float32)) * score_scale
        scores = jnp.where(visible[None], scores, -1e+30)
        row_peak = lax.optimization_barrier(jnp.max(scores, -1, keepdims=True))
        weights = jnp.where(visible[None], jnp.exp(scores - row_peak), 0.0)
        denominator = lax.optimization_barrier(jnp.sum(weights, -1))
        rounded = lax.optimization_barrier(weights.astype(jnp.bfloat16))
        mixed_heads = jnp.einsum('hqk,khd->hqd', rounded.astype(jnp.float32), values_all.astype(jnp.float32)) / denominator[..., None]
        attended = jnp.transpose(mixed_heads, (1, 0, 2)).reshape(NEW, HEADS * HD).astype(jnp.bfloat16)
        projected = jnp.zeros((NEW, D), jnp.float32)
        for group_index in range(N_TP):
            start = group_index * group_cols
            partial_value = jnp.dot(attended[:, start:start + group_cols], w_o[start:start + group_cols], preferred_element_type=jnp.float32)
            partial_value = lax.optimization_barrier(partial_value.astype(jnp.bfloat16))
            projected = projected + partial_value.astype(jnp.float32)
        hidden = (rows_in.astype(jnp.float32) + rms_scale(projected, out_gain)).astype(jnp.bfloat16)
        return (hidden, appended)
    hidden, appended = lax.map(one_request, (tokens, cache_lens, group_ids, cache_rows))
    return (hidden, appended)
```

```python
import functools

import jax
import jax.numpy as jnp
from jax import lax
from jax.experimental import pallas as pl
from jax.experimental.pallas import tpu as pltpu
from jax.sharding import PartitionSpec as P

HD = 128
HALF = HD // 2
LOG2E = 1.4426950408889634
EPS = 1e-06
VMEM = pltpu.MemorySpace.VMEM
MIB = 1024 * 1024


def proj_kernel(x_ref, wq_ref, wk_ref, wv_ref, q_ref, k_ref, v_ref, ss_ref):
    rows = x_ref[...]
    q = jnp.dot(rows, wq_ref[...], preferred_element_type=jnp.float32)
    k = jnp.dot(rows, wk_ref[...], preferred_element_type=jnp.float32)
    v = jnp.dot(rows, wv_ref[...], preferred_element_type=jnp.float32)
    q_ref[...] = q
    k_ref[...] = k
    v_ref[...] = v.astype(jnp.bfloat16)
    sq = jnp.sum(q * q, axis=-1, keepdims=True)
    sk = jnp.sum(k * k, axis=-1, keepdims=True)
    lane = lax.broadcasted_iota(jnp.int32, (rows.shape[0], HD), 1)
    both = jnp.where(lane < HALF, sq, sk)
    flipped = jnp.transpose(both)
    ss_ref[0:8] = flipped[0:8]
    ss_ref[8:16] = flipped[HALF : HALF + 8]


def project(x, w_q, w_k, w_v):
    rows, d = x.shape
    width = w_q.shape[1]
    tile = min(rows, 128)
    whole = lambda i: (0, 0)
    part = lambda i: (i, 0)
    return pl.pallas_call(
        proj_kernel,
        grid=(rows // tile,),
        in_specs=[
            pl.BlockSpec((tile, d), part),
            pl.BlockSpec((d, width), whole),
            pl.BlockSpec((d, width), whole),
            pl.BlockSpec((d, width), whole),
        ],
        out_specs=[
            pl.BlockSpec((tile, width), part),
            pl.BlockSpec((tile, width), part),
            pl.BlockSpec((tile, width), part),
            pl.BlockSpec((16, tile), lambda i: (0, i)),
        ],
        out_shape=[
            jax.ShapeDtypeStruct((rows, width), jnp.float32),
            jax.ShapeDtypeStruct((rows, width), jnp.float32),
            jax.ShapeDtypeStruct((rows, width), jnp.bfloat16),
            jax.ShapeDtypeStruct((16, rows), jnp.float32),
        ],
        compiler_params=pltpu.CompilerParams(vmem_limit_bytes=40 * MIB),
        cost_estimate=pl.CostEstimate(
            flops=2 * rows * d * width * 3, bytes_accessed=6 * d * width, transcendentals=0
        ),
        name="project",
    )(x, w_q, w_k, w_v)


def select_kernel(ids_ref, prefix_ref, out_ref):
    def one(r, carry):
        out_ref[r] = prefix_ref[ids_ref[r]]
        return carry

    lax.fori_loop(0, out_ref.shape[0], one, 0)


def select(group_ids, prefix_cache):
    count = group_ids.shape[0]
    shape = (count,) + prefix_cache.shape[1:]
    return pl.pallas_call(
        select_kernel,
        grid_spec=pltpu.PrefetchScalarGridSpec(
            num_scalar_prefetch=1,
            grid=(1,),
            in_specs=[pl.BlockSpec(prefix_cache.shape, lambda i, ids: (0, 0, 0))],
            out_specs=pl.BlockSpec(shape, lambda i, ids: (0, 0, 0)),
        ),
        out_shape=jax.ShapeDtypeStruct(shape, prefix_cache.dtype),
        name="select",
    )(group_ids, prefix_cache)


def turn(x, cos, sin):
    return x * cos + pltpu.roll(x, HALF, 1) * sin


def attend_kernel(n_tp, share, key_block, full_width, info_ref, *refs):
    q_refs = refs[:n_tp]
    k_refs = refs[n_tp : 2 * n_tp]
    v_refs = refs[2 * n_tp : 3 * n_tp]
    ss_refs = refs[3 * n_tp : 4 * n_tp]
    (cos_ref, sin_ref, qg_ref, kg_ref, cache_ref, pre_ref, out_ref, app_ref, q_ref) = refs[4 * n_tp :]
    me = info_ref[0]
    length = info_ref[1]
    new = n_tp * share
    for s in range(n_tp):
        place = pl.multiple_of(lax.rem(me + s, n_tp) * share, share)
        where = pl.ds(place, share)
        ss = ss_refs[s][...]
        cos = cos_ref[where, :]
        sin = sin_ref[where, :]
        inv = lax.rsqrt(ss * (1.0 / full_width) + EPS)
        k_inv = jnp.transpose(jnp.broadcast_to(inv[8:9], (HD, share)))
        q_inv = jnp.transpose(jnp.broadcast_to(inv[0:1] * (HD ** (-0.5) * LOG2E), (HD, share)))
        k_new = turn(k_refs[s][...] * k_inv * kg_ref[...], cos, sin).astype(jnp.bfloat16)
        app_ref[where, 0:HD] = k_new
        app_ref[where, HD : 2 * HD] = v_refs[s][...]
        q_new = turn(q_refs[s][...] * q_inv * qg_ref[...], cos, sin)
        q_ref[where, :] = q_new
    qt = jnp.transpose(q_ref[...]).astype(jnp.bfloat16)

    def scores_of(keys, queries):
        return lax.dot_general(keys, queries, (((1,), (0,)), ((), ())), preferred_element_type=jnp.float32)

    def mix(values, weights):
        return lax.dot_general(
            values,
            weights.astype(jnp.bfloat16),
            (((0,), (0,)), ((), ())),
            preferred_element_type=jnp.float32,
        )

    def absorb(state, scores, values):
        peak, total, mixed = state
        now = jnp.maximum(peak, jnp.max(scores, axis=0, keepdims=True))
        factor = jnp.exp2(peak - now)
        weights = jnp.exp2(scores - now)
        total = total * factor + jnp.sum(weights, axis=0, keepdims=True)
        mixed = mixed * factor + mix(values, weights)
        return now, total, mixed

    scores = scores_of(pre_ref[:, 0:HD], qt)
    peak = jnp.max(scores, axis=0, keepdims=True)
    weights = jnp.exp2(scores - peak)
    state = (peak, jnp.sum(weights, axis=0, keepdims=True), mix(pre_ref[:, HD : 2 * HD], weights))
    key_id = lax.broadcasted_iota(jnp.int32, (new, new), 0)
    query_id = lax.broadcasted_iota(jnp.int32, (new, new), 1)
    scores = scores_of(app_ref[:, 0:HD], qt)
    scores = jnp.where(key_id <= query_id, scores, -1e30)
    state = absorb(state, scores, app_ref[:, HD : 2 * HD])

    def step(i, state):
        at = pl.ds(pl.multiple_of(i * key_block, key_block), key_block)
        column = i * key_block + lax.broadcasted_iota(jnp.int32, (key_block, 1), 0)
        bias = jnp.where(column < length, 0.0, -1e30)
        scores = scores_of(cache_ref[at, 0:HD], qt) + bias
        return absorb(state, scores, cache_ref[at, HD : 2 * HD])

    state = lax.fori_loop(0, cache_ref.shape[0] // key_block, step, state)
    out_ref[...] = jnp.transpose(state[2] / state[1]).astype(jnp.bfloat16)


def attend(info, q, k, v, ss, cos, sin, q_gain, k_gain, cached, prefix, full_width):
    n_tp = len(q)
    share, width = q[0].shape
    new = n_tp * share
    heads = width // HD
    by_head = lambda h, info: (0, h)
    fixed = lambda h, info: (0, 0)
    key_block = min(512, cached.shape[0])
    keys = new + cached.shape[0] + prefix.shape[0]
    return pl.pallas_call(
        functools.partial(attend_kernel, n_tp, share, key_block, full_width),
        grid_spec=pltpu.PrefetchScalarGridSpec(
            num_scalar_prefetch=1,
            grid=(heads,),
            in_specs=[pl.BlockSpec((share, HD), by_head)] * (3 * n_tp)
            + [pl.BlockSpec((16, share), fixed)] * n_tp
            + [pl.BlockSpec((new, HD), fixed)] * 2
            + [pl.BlockSpec((1, HD), by_head)] * 2
            + [
                pl.BlockSpec((cached.shape[0], 2 * HD), by_head),
                pl.BlockSpec((prefix.shape[0], 2 * HD), by_head),
            ],
            out_specs=[pl.BlockSpec((new, HD), by_head), pl.BlockSpec((new, 2 * HD), by_head)],
            scratch_shapes=[pltpu.VMEM((new, HD), jnp.float32)],
        ),
        out_shape=[
            jax.ShapeDtypeStruct((new, width), jnp.bfloat16),
            jax.ShapeDtypeStruct((new, 2 * width), jnp.bfloat16),
        ],
        compiler_params=pltpu.CompilerParams(vmem_limit_bytes=40 * MIB),
        cost_estimate=pl.CostEstimate(
            flops=4 * width * new * keys,
            bytes_accessed=4 * width * keys,
            transcendentals=heads * new * keys,
        ),
        name="attend",
    )(info, *q, *k, *v, *ss, cos, sin, q_gain, k_gain, cached, prefix)


def finish_kernel(n_tp, x_ref, *refs):
    a_refs = refs[:n_tp]
    w_refs = refs[n_tp : 2 * n_tp]
    gain_ref, out_ref = refs[2 * n_tp :]
    total = None
    for a_ref, w_ref in zip(a_refs, w_refs):
        part = jnp.dot(a_ref[...], w_ref[...], preferred_element_type=jnp.float32)
        part = part.astype(jnp.bfloat16).astype(jnp.float32)
        total = part if total is None else total + part
    mean_sq = jnp.mean(total * total, axis=-1, keepdims=True)
    out_ref[...] = (
        x_ref[...].astype(jnp.float32) + total * lax.rsqrt(mean_sq + EPS) * gain_ref[...]
    ).astype(jnp.bfloat16)


def finish(x, attended, weights, out_gain):
    rows, d = x.shape
    n_tp = len(attended)
    width = attended[0].shape[1]
    tile = min(rows, 128)
    part = lambda i: (i, 0)
    whole = lambda i: (0, 0)
    return pl.pallas_call(
        functools.partial(finish_kernel, n_tp),
        grid=(rows // tile,),
        in_specs=[pl.BlockSpec((tile, d), part)]
        + [pl.BlockSpec((tile, width), part)] * n_tp
        + [pl.BlockSpec((width, d), whole)] * n_tp
        + [pl.BlockSpec((1, d), whole)],
        out_specs=pl.BlockSpec((tile, d), part),
        out_shape=jax.ShapeDtypeStruct((rows, d), jnp.bfloat16),
        compiler_params=pltpu.CompilerParams(vmem_limit_bytes=40 * MIB),
        cost_estimate=pl.CostEstimate(
            flops=2 * rows * d * width * n_tp, bytes_accessed=4 * d * width, transcendentals=0
        ),
        name="finish",
    )(x, *attended, *weights, out_gain)


def per_device(
    tokens, w_q, w_k, w_v, w_o, q_gain, k_gain, out_gain, cache_lens, group_ids, prefix_cache, cache_rows
):
    n_tp = lax.axis_size("tp")
    n_req = lax.axis_size("req")
    me = lax.axis_index("tp")
    row = lax.axis_index("req")
    width = w_q.shape[1]
    x = tokens[0]
    share = x.shape[0]
    new = share * n_tp

    def from_ahead(array, shift):
        if shift % n_tp == 0:
            return array
        return lax.ppermute(array, "tp", [((i + shift) % n_tp, i) for i in range(n_tp)])

    xs = [from_ahead(x, s) for s in range(n_tp)]
    sel = select(group_ids, prefix_cache)
    prefix = lax.all_to_all(sel, "req", 0, 0, tiled=True)
    prefix = prefix.reshape(-1, prefix.shape[-1])
    piece = w_o.shape[0] // n_req
    mine = lax.dynamic_slice_in_dim(w_o, row * piece, piece, 0)
    w_os = [w_o] + [
        lax.all_gather(from_ahead(mine, s), "req", axis=0, tiled=True) for s in range(1, n_tp)
    ]

    length = cache_lens[0]
    positions = (prefix.shape[0] + length + jnp.arange(new, dtype=jnp.int32)).astype(jnp.float32)
    exponent = jnp.arange(HALF, dtype=jnp.float32) * (-2.0 / HD)
    inverse = jnp.power(jnp.float32(500000.0), exponent)
    angles = positions[:, None] * inverse[None, :]
    cos = jnp.cos(angles)
    sin = jnp.sin(angles)
    cos = jnp.concatenate([cos, cos], -1)
    sin = jnp.concatenate([-sin, sin], -1)

    done = [project(rows, w_q, w_k, w_v) for rows in xs]
    q, k, v, ss = zip(*done)
    sums = []
    for s in range(n_tp):
        total = ss[s]
        for ahead in range(1, n_tp):
            total = total + from_ahead(ss[(s - ahead) % n_tp], ahead)
        sums.append(total)
    info = jnp.stack([me.astype(jnp.int32), length])
    attended, appended = attend(
        info, q, k, v, sums, cos, sin, q_gain[None], k_gain[None], cache_rows[0], prefix, n_tp * width
    )
    parts = []
    for s in range(n_tp):
        owner = lax.rem(me + n_tp - s, n_tp)
        rows = lax.dynamic_slice_in_dim(attended, owner * share, share, 0)
        parts.append(from_ahead(rows, s))
    hidden = finish(x, parts, w_os, out_gain[None])
    return hidden[None], appended[None]


def solution(mesh):
    return jax.shard_map(
        per_device,
        mesh=mesh,
        in_specs=(
            P("req", "tp", None),
            P(None, "tp"),
            P(None, "tp"),
            P(None, "tp"),
            P("tp", None),
            P("tp"),
            P("tp"),
            P(),
            P("req"),
            P(),
            P(None, "req", "tp"),
            P("req", None, "tp"),
        ),
        out_specs=(P("req", "tp", None), P("req", None, "tp")),
        check_vma=False,
    )
```

```python
import functools

import jax
import jax.numpy as jnp
from jax import lax
from jax.experimental import pallas as pl
from jax.experimental.pallas import tpu as pltpu
from jax.sharding import PartitionSpec as P

HD = 128
HALF = HD // 2
LOG2E = 1.4426950408889634
EPS = 1e-06
VMEM = pltpu.MemorySpace.VMEM
MIB = 1024 * 1024


def proj_kernel(x_ref, wq_ref, wk_ref, wv_ref, q_ref, k_ref, v_ref, ss_ref):
    rows = x_ref[...]
    q = jnp.dot(rows, wq_ref[...], preferred_element_type=jnp.float32)
    k = jnp.dot(rows, wk_ref[...], preferred_element_type=jnp.float32)
    v = jnp.dot(rows, wv_ref[...], preferred_element_type=jnp.float32)
    q_ref[...] = q
    k_ref[...] = k
    v_ref[...] = v.astype(jnp.bfloat16)
    sq = jnp.sum(q * q, axis=-1, keepdims=True)
    sk = jnp.sum(k * k, axis=-1, keepdims=True)
    lane = lax.broadcasted_iota(jnp.int32, (rows.shape[0], HD), 1)
    flipped = jnp.transpose(jnp.where(lane < HALF, sq, sk))
    ss = jnp.concatenate([flipped[0:8], flipped[HALF : HALF + 8]], 0)

    @pl.when(pl.program_id(0) == 0)
    def _():
        ss_ref[...] = ss

    @pl.when(pl.program_id(0) > 0)
    def _():
        ss_ref[...] += ss


def project(x, w_q, w_k, w_v):
    rows, d = x.shape
    width = w_q.shape[1]
    tile = min(width, 256)
    whole = lambda i: (0, 0)
    column = lambda i: (0, i)
    return pl.pallas_call(
        proj_kernel,
        grid=(width // tile,),
        in_specs=[pl.BlockSpec((rows, d), whole)] + [pl.BlockSpec((d, tile), column)] * 3,
        out_specs=[pl.BlockSpec((rows, tile), column)] * 3 + [pl.BlockSpec((16, rows), whole)],
        out_shape=[
            jax.ShapeDtypeStruct((rows, width), jnp.float32),
            jax.ShapeDtypeStruct((rows, width), jnp.float32),
            jax.ShapeDtypeStruct((rows, width), jnp.bfloat16),
            jax.ShapeDtypeStruct((16, rows), jnp.float32),
        ],
        compiler_params=pltpu.CompilerParams(vmem_limit_bytes=62 * MIB),
        cost_estimate=pl.CostEstimate(
            flops=2 * rows * d * width * 3, bytes_accessed=6 * d * width, transcendentals=0
        ),
        name="project",
    )(x, w_q, w_k, w_v)


def select_kernel(ids_ref, prefix_ref, out_ref):
    def one(r, carry):
        out_ref[r] = prefix_ref[ids_ref[r]]
        return carry

    lax.fori_loop(0, out_ref.shape[0], one, 0)


def select(group_ids, prefix_cache):
    count = group_ids.shape[0]
    shape = (count,) + prefix_cache.shape[1:]
    return pl.pallas_call(
        select_kernel,
        grid_spec=pltpu.PrefetchScalarGridSpec(
            num_scalar_prefetch=1,
            grid=(1,),
            in_specs=[pl.BlockSpec(prefix_cache.shape, lambda i, ids: (0, 0, 0))],
            out_specs=pl.BlockSpec(shape, lambda i, ids: (0, 0, 0)),
        ),
        out_shape=jax.ShapeDtypeStruct(shape, prefix_cache.dtype),
        compiler_params=pltpu.CompilerParams(vmem_limit_bytes=62 * MIB),
        name="select",
    )(group_ids, prefix_cache)


def turn(x, cos, sin):
    return x * cos + pltpu.roll(x, HALF, 1) * sin


def attend_kernel(n_tp, share, key_block, full_width, info_ref, *refs):
    q_refs = refs[:n_tp]
    k_refs = refs[n_tp : 2 * n_tp]
    v_refs = refs[2 * n_tp : 3 * n_tp]
    ss_refs = refs[3 * n_tp : 4 * n_tp]
    (cos_ref, sin_ref, qg_ref, kg_ref, cache_ref, pre_ref, out_ref, app_ref, q_ref) = refs[4 * n_tp :]
    me = info_ref[0]
    length = info_ref[1]
    new = n_tp * share
    for s in range(n_tp):
        place = pl.multiple_of(lax.rem(me + s, n_tp) * share, share)
        where = pl.ds(place, share)
        ss = ss_refs[s][...]
        cos = cos_ref[where, :]
        sin = sin_ref[where, :]
        inv = lax.rsqrt(ss * (1.0 / full_width) + EPS)
        k_inv = jnp.transpose(jnp.broadcast_to(inv[8:9], (HD, share)))
        q_inv = jnp.transpose(jnp.broadcast_to(inv[0:1] * (HD ** (-0.5) * LOG2E), (HD, share)))
        k_new = turn(k_refs[s][...] * k_inv * kg_ref[...], cos, sin).astype(jnp.bfloat16)
        app_ref[where, 0:HD] = k_new
        app_ref[where, HD : 2 * HD] = v_refs[s][...]
        q_new = turn(q_refs[s][...] * q_inv * qg_ref[...], cos, sin)
        q_ref[where, :] = q_new
    qt = jnp.transpose(q_ref[...]).astype(jnp.bfloat16)

    def scores_of(keys, queries):
        return lax.dot_general(keys, queries, (((1,), (0,)), ((), ())), preferred_element_type=jnp.float32)

    def mix(values, weights):
        return lax.dot_general(
            values,
            weights.astype(jnp.bfloat16),
            (((0,), (0,)), ((), ())),
            preferred_element_type=jnp.float32,
        )

    def absorb(state, scores, values):
        peak, total, mixed = state
        now = jnp.maximum(peak, jnp.max(scores, axis=0, keepdims=True))
        factor = jnp.exp2(peak - now)
        weights = jnp.exp2(scores - now)
        total = total * factor + jnp.sum(weights, axis=0, keepdims=True)
        mixed = mixed * factor + mix(values, weights)
        return now, total, mixed

    scores = scores_of(pre_ref[:, 0:HD], qt)
    peak = jnp.max(scores, axis=0, keepdims=True)
    weights = jnp.exp2(scores - peak)
    state = (peak, jnp.sum(weights, axis=0, keepdims=True), mix(pre_ref[:, HD : 2 * HD], weights))
    key_id = lax.broadcasted_iota(jnp.int32, (new, new), 0)
    query_id = lax.broadcasted_iota(jnp.int32, (new, new), 1)
    scores = scores_of(app_ref[:, 0:HD], qt)
    scores = jnp.where(key_id <= query_id, scores, -1e30)
    state = absorb(state, scores, app_ref[:, HD : 2 * HD])

    count = cache_ref.shape[0] // key_block

    def cache_scores(i):
        scores = scores_of(cache_ref[i * key_block : (i + 1) * key_block, 0:HD], qt)
        column = i * key_block + lax.broadcasted_iota(jnp.int32, (key_block, 1), 0)
        return scores + jnp.where(column < length, 0.0, -1e30)

    ahead = cache_scores(0)
    for i in range(count):
        scores = ahead
        if i + 1 < count:
            ahead = cache_scores(i + 1)
        state = absorb(state, scores, cache_ref[i * key_block : (i + 1) * key_block, HD : 2 * HD])
    out_ref[...] = jnp.transpose(state[2] / state[1]).astype(jnp.bfloat16)


def attend(info, q, k, v, ss, cos, sin, q_gain, k_gain, cached, prefix, full_width):
    n_tp = len(q)
    share, width = q[0].shape
    new = n_tp * share
    heads = width // HD
    by_head = lambda h, info: (0, h)
    fixed = lambda h, info: (0, 0)
    key_block = min(512, cached.shape[0])
    keys = new + cached.shape[0] + prefix.shape[0]
    return pl.pallas_call(
        functools.partial(attend_kernel, n_tp, share, key_block, full_width),
        grid_spec=pltpu.PrefetchScalarGridSpec(
            num_scalar_prefetch=1,
            grid=(heads,),
            in_specs=[pl.BlockSpec((share, HD), by_head)] * (3 * n_tp)
            + [pl.BlockSpec((16, share), fixed)] * n_tp
            + [pl.BlockSpec((new, HD), fixed)] * 2
            + [pl.BlockSpec((1, HD), by_head)] * 2
            + [
                pl.BlockSpec((cached.shape[0], 2 * HD), by_head),
                pl.BlockSpec((prefix.shape[0], 2 * HD), by_head),
            ],
            out_specs=[pl.BlockSpec((new, HD), by_head), pl.BlockSpec((new, 2 * HD), by_head)],
            scratch_shapes=[pltpu.VMEM((new, HD), jnp.float32)],
        ),
        out_shape=[
            jax.ShapeDtypeStruct((new, width), jnp.bfloat16),
            jax.ShapeDtypeStruct((new, 2 * width), jnp.bfloat16),
        ],
        compiler_params=pltpu.CompilerParams(vmem_limit_bytes=62 * MIB),
        cost_estimate=pl.CostEstimate(
            flops=4 * width * new * keys,
            bytes_accessed=4 * width * keys,
            transcendentals=heads * new * keys,
        ),
        name="attend",
    )(info, *q, *k, *v, *ss, cos, sin, q_gain, k_gain, cached, prefix)


def finish_kernel(n_tp, x_ref, *refs):
    own_ref = refs[0]
    a_refs = refs[1 : n_tp]
    w_refs = refs[n_tp : 2 * n_tp - 1]
    gain_ref, out_ref = refs[2 * n_tp - 1 :]
    total = own_ref[...].astype(jnp.float32)
    for a_ref, w_ref in zip(a_refs, w_refs):
        part = jnp.dot(a_ref[...], w_ref[...], preferred_element_type=jnp.float32)
        total = total + part.astype(jnp.bfloat16).astype(jnp.float32)
    mean_sq = jnp.mean(total * total, axis=-1, keepdims=True)
    out_ref[...] = (
        x_ref[...].astype(jnp.float32) + total * lax.rsqrt(mean_sq + EPS) * gain_ref[...]
    ).astype(jnp.bfloat16)


def finish(x, own, attended, weights, out_gain):
    rows, d = x.shape
    n_tp = len(attended) + 1
    width = attended[0].shape[1]
    tile = min(rows, 128)
    part = lambda i: (i, 0)
    whole = lambda i: (0, 0)
    return pl.pallas_call(
        functools.partial(finish_kernel, n_tp),
        grid=(rows // tile,),
        in_specs=[pl.BlockSpec((tile, d), part)] * 2
        + [pl.BlockSpec((tile, width), part)] * (n_tp - 1)
        + [pl.BlockSpec((width, d), whole)] * (n_tp - 1)
        + [pl.BlockSpec((1, d), whole)],
        out_specs=pl.BlockSpec((tile, d), part),
        out_shape=jax.ShapeDtypeStruct((rows, d), jnp.bfloat16),
        compiler_params=pltpu.CompilerParams(vmem_limit_bytes=62 * MIB),
        cost_estimate=pl.CostEstimate(
            flops=2 * rows * d * width * n_tp, bytes_accessed=4 * d * width, transcendentals=0
        ),
        name="finish",
    )(x, own, *attended, *weights, out_gain)


def angles(start, count):
    positions = (start + jnp.arange(count, dtype=jnp.int32)).astype(jnp.float32)
    exponent = jnp.arange(HALF, dtype=jnp.float32) * (-2.0 / HD)
    inverse = jnp.power(jnp.float32(500000.0), exponent)
    turns = positions[:, None] * inverse[None, :]
    cos = jnp.cos(turns)
    sin = jnp.sin(turns)
    return jnp.concatenate([cos, cos], -1), jnp.concatenate([-sin, sin], -1)


def per_device(
    tokens, w_q, w_k, w_v, w_o, q_gain, k_gain, out_gain, cache_lens, group_ids, prefix_cache, cache_rows
):
    n_tp = lax.axis_size("tp")
    n_req = lax.axis_size("req")
    me = lax.axis_index("tp")
    row = lax.axis_index("req")
    width = w_q.shape[1]
    x = tokens[0]
    share = x.shape[0]
    new = share * n_tp

    def from_ahead(array, shift):
        if shift % n_tp == 0:
            return array
        return lax.ppermute(array, "tp", [((i + shift) % n_tp, i) for i in range(n_tp)])

    xs = [from_ahead(x, s) for s in range(n_tp)]
    sel = select(group_ids, prefix_cache)
    prefix = lax.all_to_all(sel, "req", 0, 0, tiled=True)
    prefix = prefix.reshape(-1, prefix.shape[-1])
    cos, sin = angles(prefix.shape[0] + cache_lens[0], new)
    first = project(x, w_q, w_k, w_v)
    piece = w_o.shape[0] // n_req
    mine = lax.dynamic_slice_in_dim(w_o, row * piece, piece, 0)
    xs, mine, prefix, cos, sin, first = lax.optimization_barrier((xs, mine, prefix, cos, sin, first))
    done = [first] + [project(rows, w_q, w_k, w_v) for rows in xs[1:]]
    pieces, done = lax.optimization_barrier(([from_ahead(mine, s) for s in range(1, n_tp)], done))
    w_os = [w_o] + [lax.all_gather(one, "req", axis=0, tiled=True) for one in pieces]
    length = cache_lens[0]
    q, k, v, ss = zip(*done)
    sums = []
    for s in range(n_tp):
        total = ss[s]
        for ahead in range(1, n_tp):
            total = total + from_ahead(ss[(s - ahead) % n_tp], ahead)
        sums.append(total)
    info = jnp.stack([me.astype(jnp.int32), length])
    attended, appended = attend(
        info, q, k, v, sums, cos, sin, q_gain[None], k_gain[None], cache_rows[0], prefix, n_tp * width
    )
    parts = []
    for s in range(n_tp):
        owner = lax.rem(me + n_tp - s, n_tp)
        rows = lax.dynamic_slice_in_dim(attended, owner * share, share, 0)
        parts.append(from_ahead(rows, s))
    own = jnp.dot(parts[0], w_o, preferred_element_type=jnp.float32).astype(jnp.bfloat16)
    hidden = finish(x, own, parts[1:], w_os[1:], out_gain[None])
    return hidden[None], appended[None]


def solution(mesh):
    return jax.shard_map(
        per_device,
        mesh=mesh,
        in_specs=(
            P("req", "tp", None),
            P(None, "tp"),
            P(None, "tp"),
            P(None, "tp"),
            P("tp", None),
            P("tp"),
            P("tp"),
            P(),
            P("req"),
            P(),
            P(None, "req", "tp"),
            P("req", None, "tp"),
        ),
        out_specs=(P("req", "tp", None), P("req", None, "tp")),
        check_vma=False,
    )
```
